32 devices in a mesh: seq: 4 (over z), expert: 8 (over y, x, core).
Axes of the slice: x: 2, y: 2, z: 4, core: 2. Of those that a mesh axis runs over, the one named last changes fastest.
Arguments:
- tokens: bfloat16 [4096, 4096], P(('seq', 'expert')), may hold values from -6 to 6
- routes: int32 [4096, 8], P(('seq', 'expert')), may hold values from 0 to 31, all different within a row; in each aligned block of 128 rows (0 to 127, 128 to 255, ...) at most 40 rows name the same one
- gates: bfloat16 [4096, 8], P(('seq', 'expert')), may hold values from 0.049804688 to 0.59765625
- w_gate: bfloat16 [32, 4096, 768], P(('seq', 'expert')), may hold values from -0.09375 to 0.09375
- w_up: bfloat16 [32, 4096, 768], P(('seq', 'expert')), may hold values from -0.09375 to 0.09375
- w_down: bfloat16 [32, 768, 4096], P(('seq', 'expert')), may hold values from -0.21875 to 0.21875
Outputs:
- mixed: bfloat16 [4096, 4096], P(('seq', 'expert'))
The draws below stay inside these ranges and needn't reach their ends.
Inputs may be any that keep to these rules, and one draw needn't show every extreme that they name: `routes`: within the rows of one device (aligned blocks of 128 rows) no expert is named by more than 40 rows, a bound that some block reaches; each row names 8 different experts; expert e is held by the device of index e along seq+expert.
All inputs are finite; a program needn't handle non-finite values.
Results may differ from the reference program's by a relative error of at most 0.0057.
Values may be sent and summed in bfloat16 or wider, within the bound.
No kernel may reach another device: no remote copies, remote signals or barrier semaphores. Data moves between devices by JAX's collectives and lax.ppermute only.
A program may use at most 128 MiB of HBM per device.

```python
import math
import jax
import jax.numpy as jnp
import numpy as np
from jax import lax

D = 4096
TOP = 8
FF = 768
TOK_DEV = 128
EXPERTS = 32
CAP = 40
TOKENS = 4096


def steps_of(key, extent, shards, smallest, high):
    level, own = 1.0, jax.random.fold_in(key, 6)
    for position, parts in shards:
        steps = jnp.exp(jax.random.uniform(jax.random.fold_in(own, position), (parts,), jnp.float32, smallest / len(shards), high / len(shards)))
        level = level * jnp.repeat(steps, extent[position] // parts).reshape([-1 if axis == position else 1 for axis in range(len(extent))])
    return level


def routed_block(stream_key, own, number, rows, amount, top, most, skew):
    order = jax.random.permutation(stream_key, amount)
    crowded, ordinary = shares(amount, rows * top, most, skew, True), shares(amount, rows * top, most, skew, False)
    places = jnp.arange(amount)

    def named(tallies, offset_by):
        used = int((tallies > 0).sum())
        fixed = max(1, used // 4)
        passed = fixed + (places - fixed + offset_by * (used - fixed)) % max(1, amount - fixed)
        return jnp.zeros((amount,), jnp.int32).at[order[jnp.where(places < fixed, places, passed)]].set(jnp.asarray(tallies, jnp.int32))

    tallies = jnp.where(number % 4 == 0, named(crowded, number // 4), named(ordinary, number - number // 4 - 1))
    mixed = jax.random.permutation(jax.random.fold_in(own, 3), amount)
    giver, taker = mixed[0:amount // 2 * 2:2], mixed[1:amount // 2 * 2:2]
    margin = jnp.minimum(tallies[giver] - 1, most - tallies[taker]) // 2
    margin = jnp.where((giver == order[0]) | (taker == order[0]) | (tallies[taker] == 0), 0, jnp.maximum(margin, 0))
    passed = jax.random.randint(jax.random.fold_in(own, 4), (amount // 2,), 0, 1 << 20) % (margin + 1)
    tallies = tallies.at[giver].add(-passed).at[taker].add(passed)
    members = jnp.searchsorted(jnp.cumsum(tallies), jnp.arange(rows * top), side="right").astype(jnp.int32)
    grid = members.reshape(top, rows).T
    grid = grid[jax.random.permutation(jax.random.fold_in(own, 1), rows)]
    offset_by = jax.random.randint(jax.random.fold_in(own, 2), (rows, 1), 0, top)
    return jnp.take_along_axis(grid, (jnp.arange(top)[None, :] + offset_by) % top, axis=1)


def shares(number_of, total, reach, skew, full):
    weights = [(1 << 20) // math.isqrt(rank ** skew) + 1 for rank in range(1, number_of + 1)]
    largest = reach if full else min(reach, max(-(-total // number_of), total * weights[0] // sum(weights)))
    least = 1 if total - largest >= number_of - 1 else 0
    holding, surplus = [largest] + [least] * (number_of - 1), total - largest - least * (number_of - 1)
    while surplus > 0:
        candidates = [i for i in range(1, number_of) if holding[i] < largest] or [i for i in range(1, number_of) if holding[i] < reach]
        mass, budget = sum([weights[i] for i in candidates]), surplus
        for i in candidates:
            addition = min(reach - holding[i], max(1, budget * weights[i] // mass), surplus)
            holding[i] = holding[i] + addition
            surplus = surplus - addition
    return np.array(holding)


def scatter_about(stream_key, shape, deviation, most, cuts=(), held_as=jnp.bfloat16):
    array = deviation * jax.random.normal(stream_key, shape, jnp.float32)
    if cuts:
        array = array * steps_of(stream_key, shape, cuts, -0.22, 0.18)
    return jnp.clip(array, -most, most).astype(held_as)


def setup_inputs(seed: int = 0) -> dict:
    splits = jax.random.split(jax.random.key(seed), 7)
    tokens = scatter_about(splits[0], (TOKENS, D), 1.0, 6.0, ((0, 32),))
    routes_keys = jax.random.split(jax.random.fold_in(splits[1], 1), TOKENS // TOK_DEV)
    routes_turns = jax.random.permutation(jax.random.fold_in(splits[1], 3), TOKENS // TOK_DEV)
    routes = jax.vmap(lambda own, number: routed_block(jax.random.fold_in(splits[1], 2), own, number, TOK_DEV, EXPERTS, TOP, CAP, 2))(routes_keys, routes_turns).reshape((TOKENS, TOP))
    gates = jnp.clip(jnp.exp(math.log(0.59765625) - 2.4849066 * jax.random.uniform(splits[2], (TOKENS, TOP), jnp.float32) ** steps_of(splits[2], (TOKENS, TOP), ((0, 32),), -0.2, 0.2)), 0.049804688, 0.59765625).astype(jnp.bfloat16)
    w_gate = scatter_about(splits[3], (EXPERTS, D, FF), D ** -0.5, 0.09375, ((0, 32),))
    w_up = scatter_about(splits[4], (EXPERTS, D, FF), D ** -0.5, 0.09375, ((0, 32),))
    w_down = scatter_about(splits[5], (EXPERTS, FF, D), FF ** -0.5, 0.21875, ((0, 32),))
    return {"tokens": tokens, "routes": routes, "gates": gates, "w_gate": w_gate, "w_up": w_up, "w_down": w_down}


def expert_output(row_block, gate_matrix, up_matrix, down_matrix):
    gate_act = jnp.dot(row_block, gate_matrix, preferred_element_type=jnp.float32)
    up_act = jnp.dot(row_block, up_matrix, preferred_element_type=jnp.float32)
    hidden = (jax.nn.silu(gate_act) * up_act).astype(jnp.bfloat16)
    return jnp.dot(hidden, down_matrix, preferred_element_type=jnp.float32).astype(jnp.bfloat16)


def reference(tokens, routes, gates, w_gate, w_up, w_down):
    total_rows = tokens.shape[0]
    fanout = routes.shape[1]
    features = tokens.shape[1]
    limit = EXPERTS * CAP
    flat_routes = routes.reshape(-1).astype(jnp.int32)
    flat_gates = jnp.concatenate([gates.reshape(-1), jnp.zeros((1,), gates.dtype)], 0)
    padded = jnp.concatenate([tokens, jnp.zeros((1, features), tokens.dtype)], 0)

    def one_expert(running, inputs):
        expert, gate_matrix, up_matrix, down_matrix = inputs
        picked_ids = jnp.nonzero(flat_routes == expert, size=limit, fill_value=total_rows * fanout)[0].astype(jnp.int32)
        token_ids = (picked_ids // fanout).astype(jnp.int32)
        row_block = jnp.take(padded, token_ids, axis=0)
        outputs = expert_output(row_block, gate_matrix, up_matrix, down_matrix)
        weights = jnp.take(flat_gates, picked_ids, axis=0).astype(jnp.float32)
        running = running.at[token_ids].add(weights[:, None] * outputs.astype(jnp.float32))
        return running, None

    start = jnp.zeros((total_rows + 1, features), jnp.float32)
    expert_ids = jnp.arange(EXPERTS, dtype=jnp.int32)
    final, unused = lax.scan(one_expert, start, (expert_ids, w_gate, w_up, w_down))
    return final[:total_rows].astype(jnp.bfloat16)
```

```python
import functools
import math

import jax
import jax.numpy as jnp
import numpy as np
from jax import lax
from jax.experimental import pallas as pl
from jax.experimental.pallas import tpu as pltpu
from jax.sharding import PartitionSpec as P

AXES = ("seq", "expert")
F32 = jnp.float32
BF16 = jnp.bfloat16
VMEM_LIMIT = 56 * 1024 * 1024


class Grid:
    def __init__(self, seq, plane):
        side = math.isqrt(plane)
        if side * side == plane:
            self.cores = 1
        else:
            self.cores = 2
            side = math.isqrt(plane // 2)
        self.seq, self.plane, self.side = seq, plane, side
        self.count = seq * plane

    def split(self, p):
        k = p % self.cores
        return p // self.cores // self.side, p // self.cores % self.side, k

    def join(self, i, j, k):
        return (i * self.side + j) * self.cores + k

    def first(self, p, b):
        i, j, k = self.split(p)
        return self.join(i, j ^ b, k) if k % 2 == 0 else self.join(i ^ b, j, k)

    def second(self, p, b, kc):
        i, j, k = self.split(p)
        return self.join(i ^ b, j, k ^ kc) if k % 2 == 0 else self.join(i, j ^ b, k ^ kc)

    def in_plane(self, move):
        return [(z * self.plane + p, z * self.plane + move(p)) for z in range(self.seq) for p in range(self.plane)]

    def along_seq(self, pairs):
        return [(s * self.plane + p, d * self.plane + p) for s, d in pairs for p in range(self.plane)]

    def slots(self):
        if self.seq == 4:
            sources = [[0, 1, 2, 3], [1, 0, 3, 2], [2, 2, 1, 1], [3, 3, 0, 0]]
            near, middle, ends = [(0, 1), (1, 0), (2, 3), (3, 2)], [(1, 2), (2, 1)], [(1, 0), (2, 3)]
            relays = [[], [(0, near)], [(0, middle), (2, ends)], [(1, middle), (3, ends)]]
        else:
            sources = [[z ^ s for z in range(self.seq)] for s in range(self.seq)]
            relays = [[]] + [[(0, [(z, z ^ s) for z in range(self.seq)])] for s in range(1, self.seq)]
        return sources, relays


def back(pairs):
    return [(d, s) for s, d in pairs]


def move(x, pairs):
    return lax.ppermute(x, AXES, pairs)


def codes(meta, experts, base, want_gates):
    meta = meta.astype(F32)
    fanout = meta.shape[0] // 2
    tokens = meta.shape[1]
    routes, gates = meta[:fanout], meta[fanout:]
    height = -(-len(experts) // 8) * 8
    line = lax.broadcasted_iota(jnp.int32, (height, tokens), 0)
    named = jnp.zeros((height, tokens), F32)
    weights = []
    for n, e in enumerate(experts):
        hit = routes == e.astype(F32)
        named = jnp.where(line == n, jnp.max(jnp.where(hit, 1.0, 0.0), axis=0, keepdims=True), named)
        if want_gates:
            weights.append(jnp.sum(jnp.where(hit, gates, 0.0), axis=0, keepdims=True))
    before = lax.broadcasted_iota(jnp.int32, (tokens, tokens), 0) < lax.broadcasted_iota(jnp.int32, (tokens, tokens), 1)
    rank = jnp.dot(named.astype(BF16), jnp.where(before, 1.0, 0.0).astype(BF16), preferred_element_type=F32)
    rows = jnp.where(named > 0, rank + base, -1.0).astype(jnp.int32)
    return [rows[n : n + 1] for n in range(len(experts))], weights


def select_kernel(grid, slot, cap, ids, *refs):
    a, outs = grid.side, grid.side * grid.cores
    metas, toks, results = refs[:a], refs[a : 2 * a], refs[2 * a :]
    experts = [ids[grid.seq * a + n] for n in range(outs)]
    total = [None] * outs
    for src in range(a):
        rows, _ = codes(metas[src][...], experts, src * cap, False)
        values = toks[src][...]
        line = lax.broadcasted_iota(jnp.int32, (a * cap, values.shape[0]), 0)
        for n in range(outs):
            onehot = jnp.where(line == rows[n], 1.0, 0.0).astype(BF16)
            part = jnp.dot(onehot, values, preferred_element_type=F32)
            total[n] = part if src == 0 else total[n] + part
    for n in range(outs):
        results[n][...] = total[n].astype(BF16)


def meta_spec(slot, a, src, meta):
    return pl.BlockSpec((None,) + meta.shape[1:], lambda d, ids: (ids[slot * a + src], 0, 0))


def select(grid, slot, cap, ids, meta, toks):
    a, outs = grid.side, grid.side * grid.cores
    rows, width = toks[0].shape
    tile = min(width, 1024)
    return pl.pallas_call(
        functools.partial(select_kernel, grid, slot, cap),
        grid_spec=pltpu.PrefetchScalarGridSpec(
            num_scalar_prefetch=1,
            grid=(width // tile,),
            in_specs=[meta_spec(slot, a, src, meta) for src in range(a)]
            + [pl.BlockSpec((rows, tile), lambda d, ids: (0, d)) for _ in range(a)],
            out_specs=[pl.BlockSpec((a * cap, tile), lambda d, ids: (0, d)) for _ in range(outs)],
        ),
        out_shape=[jax.ShapeDtypeStruct((a * cap, width), BF16) for _ in range(outs)],
        compiler_params=pltpu.CompilerParams(vmem_limit_bytes=VMEM_LIMIT),
        cost_estimate=pl.CostEstimate(
            flops=2 * outs * a * a * cap * rows * width,
            bytes_accessed=2 * width * (a * rows + outs * a * cap),
            transcendentals=0,
        ),
        name="select",
    )(ids, *([meta] * a), *toks)


def mix_kernel(grid, slot, cap, sources, extras, ids, *refs):
    a, ins = grid.side, grid.side * grid.cores
    metas, refs = refs[: len(sources)], refs[len(sources) :]
    blocks, refs = refs[:ins], refs[ins:]
    added, results = refs[:extras], refs[extras:]
    experts = [ids[grid.seq * a + n] for n in range(ins)]
    for at, src in enumerate(sources):
        rows, weights = codes(metas[at][...], experts, src * cap, True)
        line = lax.broadcasted_iota(jnp.int32, (a * cap, rows[0].shape[1]), 0)
        total = None
        for n in range(ins):
            spread = jnp.where(line == rows[n], weights[n], 0.0).astype(BF16)
            part = lax.dot_general(spread, blocks[n][...], (((0,), (0,)), ((), ())), preferred_element_type=F32)
            total = part if total is None else total + part
        for ref in added:
            total = total + ref[...].astype(F32)
        results[at][...] = total.astype(BF16)


def mix(grid, slot, cap, ids, meta, blocks, sources, extras=()):
    a, ins = grid.side, grid.side * grid.cores
    rows, width = meta.shape[2], blocks[0].shape[1]
    tile = min(width, 1024)
    wide = pl.BlockSpec((rows, tile), lambda d, ids: (0, d))
    return pl.pallas_call(
        functools.partial(mix_kernel, grid, slot, cap, sources, len(extras)),
        grid_spec=pltpu.PrefetchScalarGridSpec(
            num_scalar_prefetch=1,
            grid=(width // tile,),
            in_specs=[meta_spec(slot, a, src, meta) for src in sources]
            + [pl.BlockSpec((a * cap, tile), lambda d, ids: (0, d)) for _ in blocks]
            + [wide for _ in extras],
            out_specs=[wide for _ in sources],
        ),
        out_shape=[jax.ShapeDtypeStruct((rows, width), BF16) for _ in sources],
        compiler_params=pltpu.CompilerParams(vmem_limit_bytes=VMEM_LIMIT),
        cost_estimate=pl.CostEstimate(
            flops=2 * len(sources) * ins * a * cap * rows * width,
            bytes_accessed=2 * width * (ins * a * cap + rows * (len(extras) + len(sources))),
            transcendentals=0,
        ),
        name="mix",
    )(ids, *([meta] * len(sources)), *blocks, *extras)


def expert_kernel(count, *refs):
    ins, (wg, wu, wd), outs, (x, total) = refs[:count], refs[count : count + 3], refs[count + 3 : 2 * count + 3], refs[2 * count + 3 :]
    step = pl.program_id(0)
    height = ins[0].shape[0]

    @pl.when(step == 0)
    def _():
        x[...] = jnp.concatenate([r[...] for r in ins], axis=0)

    rows = x[...]
    gate = jnp.dot(rows, wg[...], preferred_element_type=F32)
    up = jnp.dot(rows, wu[...], preferred_element_type=F32)
    hidden = (gate / (1.0 + jnp.exp(-gate)) * up).astype(BF16)
    width = total.shape[1]
    piece = min(width, 1024)

    for at in range(0, width, piece):
        part = jnp.dot(hidden, wd[:, at : at + piece], preferred_element_type=F32)

        @pl.when(step == 0)
        def _():
            total[:, at : at + piece] = part

        @pl.when(step > 0)
        def _():
            total[:, at : at + piece] += part

    @pl.when(step == pl.num_programs(0) - 1)
    def _():
        for n, r in enumerate(outs):
            r[...] = total[n * height : (n + 1) * height, :].astype(BF16)


def expert(blocks, w_gate, w_up, w_down):
    count = len(blocks)
    height, width = blocks[0].shape
    depth = w_gate.shape[2]
    tile = 256 if depth % 256 == 0 else depth
    whole = pl.BlockSpec((height, width), lambda f: (0, 0))
    return pl.pallas_call(
        functools.partial(expert_kernel, count),
        grid=(depth // tile,),
        in_specs=[whole] * count
        + [
            pl.BlockSpec((None, width, tile), lambda f: (0, 0, f)),
            pl.BlockSpec((None, width, tile), lambda f: (0, 0, f)),
            pl.BlockSpec((None, tile, width), lambda f: (0, f, 0)),
        ],
        out_specs=[whole] * count,
        out_shape=[jax.ShapeDtypeStruct((height, width), BF16)] * count,
        scratch_shapes=[pltpu.VMEM((count * height, width), BF16), pltpu.VMEM((count * height, width), F32)],
        compiler_params=pltpu.CompilerParams(vmem_limit_bytes=VMEM_LIMIT),
        cost_estimate=pl.CostEstimate(
            flops=6 * count * height * width * depth,
            bytes_accessed=6 * width * depth + 4 * count * height * width,
            transcendentals=count * height * depth,
        ),
        name="expert",
    )(*blocks, w_gate, w_up, w_down)


def local(grid, tokens, routes, gates, w_gate, w_up, w_down):
    tok_rows, _ = tokens.shape
    fanout = routes.shape[1]
    cap = tok_rows * fanout * 5 // (4 * grid.count)
    a, c = grid.side, grid.cores
    sources, relays = grid.slots()

    table = np.zeros((grid.count, grid.seq * a + a * c), np.int32)
    for z in range(grid.seq):
        for p in range(grid.plane):
            row = [sources[s][z] * grid.plane + grid.first(p, b) for s in range(grid.seq) for b in range(a)]
            row += [z * grid.plane + grid.second(p, b, kc) for b in range(a) for kc in range(c)]
            table[z * grid.plane + p] = row
    ids = lax.dynamic_index_in_dim(jnp.asarray(table), lax.axis_index(AXES), 0, keepdims=False)

    hop1 = [None] + [grid.in_plane(lambda p, b=b: grid.first(p, b)) for b in range(1, a)]
    hop2 = [grid.in_plane(lambda p, b=b, kc=kc: grid.second(p, b, kc)) for b in range(a) for kc in range(c)]

    own_meta = jnp.concatenate([routes.astype(BF16), gates], axis=1).T
    meta = lax.all_gather(own_meta, AXES, axis=0, tiled=False)

    seq_index = lax.axis_index("seq")
    held = [tokens]
    for s in range(1, grid.seq):
        got = None
        for origin, pairs in relays[s]:
            arrived = move(got if origin == s else held[origin], grid.along_seq(pairs))
            if got is None:
                got = arrived
            else:
                reached = functools.reduce(jnp.logical_or, [seq_index == d for _, d in pairs])
                got = jnp.where(reached, arrived, got)
        held.append(got)

    returned = []
    for s in range(grid.seq):
        near = [held[s]] + [move(held[s], hop1[b]) for b in range(1, a)]
        rows = select(grid, s, cap, ids, meta, near)
        rows = [rows[0]] + [move(rows[n], hop2[n]) for n in range(1, a * c)]
        outs = expert(rows, w_gate, w_up, w_down)
        returned.append([outs[0]] + [move(outs[n], back(hop2[n])) for n in range(1, a * c)])

    inbox = [[] for _ in range(grid.seq)]
    for s in reversed(range(grid.seq)):
        sums = mix(grid, s, cap, ids, meta, returned[s], list(range(1, a)))
        extras = [move(sums[b - 1], hop1[b]) for b in range(1, a)] + inbox[s]
        (part,) = mix(grid, s, cap, ids, meta, returned[s], [0], extras)
        if s == 0:
            return part
        for origin, pairs in reversed(relays[s]):
            arrived = move(part, grid.along_seq(back(pairs)))
            if origin == s:
                part = (part.astype(F32) + arrived.astype(F32)).astype(BF16)
            else:
                inbox[origin].append(arrived)


def solution(mesh):
    grid = Grid(mesh.shape["seq"], mesh.shape["expert"])
    two, three = P(AXES, None), P(AXES, None, None)
    return jax.shard_map(
        functools.partial(local, grid),
        mesh=mesh,
        in_specs=(two, two, two, three, three, three),
        out_specs=two,
        check_vma=False,
    )
```

```python
import functools
import math

import jax
import jax.numpy as jnp
import numpy as np
from jax import lax
from jax.experimental import pallas as pl
from jax.experimental.pallas import tpu as pltpu
from jax.sharding import PartitionSpec as P

AXES = ("seq", "expert")
F32 = jnp.float32
BF16 = jnp.bfloat16
VMEM_LIMIT = 56 * 1024 * 1024
TILE = 2048
SHORT = pl.CostEstimate(flops=2_000_000_000, bytes_accessed=6_000_000, transcendentals=0)
LONG = pl.CostEstimate(flops=6_000_000_000, bytes_accessed=24_000_000, transcendentals=0)


class Grid:
    def __init__(self, seq, plane):
        side = math.isqrt(plane)
        if side * side == plane:
            self.cores = 1
        else:
            self.cores = 2
            side = math.isqrt(plane // 2)
        self.seq, self.plane, self.side = seq, plane, side
        self.count = seq * plane

    def split(self, p):
        k = p % self.cores
        return p // self.cores // self.side, p // self.cores % self.side, k

    def join(self, i, j, k):
        return (i * self.side + j) * self.cores + k

    def first(self, p, b):
        i, j, k = self.split(p)
        return self.join(i, j ^ b, k) if k % 2 == 0 else self.join(i ^ b, j, k)

    def second(self, p, b, kc):
        i, j, k = self.split(p)
        return self.join(i ^ b, j, k ^ kc) if k % 2 == 0 else self.join(i, j ^ b, k ^ kc)

    def in_plane(self, move):
        return [(z * self.plane + p, z * self.plane + move(p)) for z in range(self.seq) for p in range(self.plane)]

    def along_seq(self, pairs):
        return [(s * self.plane + p, d * self.plane + p) for s, d in pairs for p in range(self.plane)]

    def relays(self):
        if self.seq == 4:
            near, middle, ends = [(0, 1), (1, 0), (2, 3), (3, 2)], [(1, 2), (2, 1)], [(1, 0), (2, 3)]
            return [[], [(0, near)], [(0, middle), (2, ends)], [(1, middle), (3, ends)]]
        return [[]] + [[(0, [(z, z ^ s) for z in range(self.seq)])] for s in range(1, self.seq)]


    def returns(self):
        if self.seq == 4:
            near, middle, ends = [(0, 1), (1, 0), (2, 3), (3, 2)], [(1, 2), (2, 1)], [(0, 1), (3, 2)]
            return [[], [near], [ends, middle], [ends, [(1, 3), (2, 0)]]]
        return [[]] + [[[(z, z ^ s) for z in range(self.seq)]] for s in range(1, self.seq)]


def back(pairs):
    return [(d, s) for s, d in pairs]


def move(x, pairs):
    return lax.ppermute(x, AXES, pairs)


def pin_kernel(*refs):
    pass


def pin(values, event, us=0):
    count = len(values)
    anywhere = pl.BlockSpec(memory_space=pl.ANY)
    return pl.pallas_call(
        pin_kernel,
        in_specs=[anywhere] * (count + 1),
        out_specs=[anywhere] * count,
        out_shape=[jax.ShapeDtypeStruct(v.shape, v.dtype) for v in values],
        input_output_aliases={n: n for n in range(count)},
        cost_estimate=pl.CostEstimate(flops=int(us * 1e9), bytes_accessed=int(us * 3e6), transcendentals=0),
        name="pin",
    )(*values, event)


def codes(meta, experts, base, want_gates):
    meta = meta.astype(F32)
    fanout = meta.shape[0] // 2
    tokens = meta.shape[1]
    routes, gates = meta[:fanout], meta[fanout:]
    height = -(-len(experts) // 8) * 8
    line = lax.broadcasted_iota(jnp.int32, (height, tokens), 0)
    named = jnp.zeros((height, tokens), F32)
    weights = jnp.zeros((height, tokens), F32)
    for n, e in enumerate(experts):
        hit = routes == e.astype(F32)
        named = jnp.where(line == n, jnp.max(jnp.where(hit, 1.0, 0.0), axis=0, keepdims=True), named)
        if want_gates:
            weights = jnp.where(line == n, jnp.sum(jnp.where(hit, gates, 0.0), axis=0, keepdims=True), weights)
    before = lax.broadcasted_iota(jnp.int32, (tokens, tokens), 0) < lax.broadcasted_iota(jnp.int32, (tokens, tokens), 1)
    rank = jnp.dot(named.astype(BF16), jnp.where(before, 1.0, 0.0).astype(BF16), preferred_element_type=F32)
    return jnp.where(named > 0, rank + base, -1.0), weights


def select_kernel(grid, cap, ids, *refs):
    a, outs = grid.side, grid.side * grid.cores
    metas, toks, results, table = refs[:a], refs[a : 2 * a], refs[-outs - 1 : -1], refs[-1]

    @pl.when(pl.program_id(0) == 0)
    def _():
        experts = [ids[n] for n in range(outs)]
        for src in range(a):
            rows, _ = codes(metas[src][...], experts, src * cap, False)
            line = lax.broadcasted_iota(jnp.int32, (a * cap, rows.shape[1]), 0).astype(F32)
            for n in range(outs):
                table[src, n] = jnp.where(line == rows[n : n + 1], 1.0, 0.0).astype(BF16)

    for n in range(outs):
        total = jnp.dot(table[0, n], toks[0][...], preferred_element_type=F32)
        for src in range(1, a):
            total = total + jnp.dot(table[src, n], toks[src][...], preferred_element_type=F32)
        results[n][...] = total.astype(BF16)


def meta_spec(tok, width, lines):
    rows = tok.shape[0]
    return pl.BlockSpec((lines, rows), lambda d, ids: (0, width // rows))


def select(grid, cap, ids, lines, width, toks, events=()):
    a, outs = grid.side, grid.side * grid.cores
    rows = toks[0].shape[0]
    tile = min(width, TILE)
    return pl.pallas_call(
        functools.partial(select_kernel, grid, cap),
        grid_spec=pltpu.PrefetchScalarGridSpec(
            num_scalar_prefetch=1,
            grid=(width // tile,),
            in_specs=[meta_spec(tok, width, lines) for tok in toks]
            + [pl.BlockSpec((rows, tile), lambda d, ids: (0, d)) for _ in range(a)]
            + [pl.BlockSpec(memory_space=pl.ANY) for _ in events],
            out_specs=[pl.BlockSpec((a * cap, tile), lambda d, ids: (0, d)) for _ in range(outs)],
            scratch_shapes=[pltpu.VMEM((a, outs, a * cap, rows), BF16)],
        ),
        out_shape=[jax.ShapeDtypeStruct((a * cap, width), BF16) for _ in range(outs)],
        compiler_params=pltpu.CompilerParams(vmem_limit_bytes=VMEM_LIMIT),
        cost_estimate=SHORT,
        name="select",
    )(ids, *toks, *toks, *events)


def mix_kernel(grid, cap, sources, extras, ids, *refs):
    a, ins = grid.side, grid.side * grid.cores
    metas, refs = refs[: len(sources)], refs[len(sources) :]
    blocks, refs = refs[:ins], refs[ins:]
    added, results, table = refs[:extras], refs[-len(sources) - 1 : -1], refs[-1]

    @pl.when(pl.program_id(0) == 0)
    def _():
        experts = [ids[n] for n in range(ins)]
        for at, src in enumerate(sources):
            rows, weights = codes(metas[at][...], experts, src * cap, True)
            rows, weights = rows.T, weights.T
            line = lax.broadcasted_iota(jnp.int32, (rows.shape[0], a * cap), 1).astype(F32)
            for n in range(ins):
                spread = jnp.where(line == rows[:, n : n + 1], weights[:, n : n + 1], 0.0)
                table[at, n] = spread.astype(BF16)

    for at in range(len(sources)):
        total = jnp.dot(table[at, 0], blocks[0][...], preferred_element_type=F32)
        for n in range(1, ins):
            total = total + jnp.dot(table[at, n], blocks[n][...], preferred_element_type=F32)
        for ref in added:
            total = total + ref[...].astype(F32)
        results[at][...] = total.astype(BF16)


def mix(grid, cap, ids, lines, toks, blocks, sources, extras=(), events=()):
    a, ins = grid.side, grid.side * grid.cores
    rows, width = toks[0].shape[0], blocks[0].shape[1]
    tile = min(width, TILE)
    wide = pl.BlockSpec((rows, tile), lambda d, ids: (0, d))
    return pl.pallas_call(
        functools.partial(mix_kernel, grid, cap, sources, len(extras)),
        grid_spec=pltpu.PrefetchScalarGridSpec(
            num_scalar_prefetch=1,
            grid=(width // tile,),
            in_specs=[meta_spec(toks[src], width, lines) for src in sources]
            + [pl.BlockSpec((a * cap, tile), lambda d, ids: (0, d)) for _ in blocks]
            + [wide for _ in extras]
            + [pl.BlockSpec(memory_space=pl.ANY) for _ in events],
            out_specs=[wide for _ in sources],
            scratch_shapes=[pltpu.VMEM((len(sources), ins, rows, a * cap), BF16)],
        ),
        out_shape=[jax.ShapeDtypeStruct((rows, width), BF16) for _ in sources],
        compiler_params=pltpu.CompilerParams(vmem_limit_bytes=VMEM_LIMIT),
        cost_estimate=SHORT,
        name="mix",
    )(ids, *[toks[src] for src in sources], *blocks, *extras, *events)


def expert_kernel(count, pieces, *refs):
    ins, (wg, wu, wd), outs = refs[:count], refs[count : count + 3], refs[-count - 8 : -8]
    x, wg_in, wu_in, wd_in, gate, up, sems, x_sems = refs[-8:]
    height = ins[0].shape[0]
    width, depth = wg.shape[1:]
    piece = width // pieces
    copies = []
    for n, r in enumerate(ins):
        copies.append(pltpu.make_async_copy(r, x.at[n], x_sems.at[n]))
    for at in range(pieces):
        part = pl.ds(at * piece, piece)
        copies.append(pltpu.make_async_copy(wg.at[0, part], wg_in.at[part], sems.at[at]))
        copies.append(pltpu.make_async_copy(wu.at[0, part], wu_in.at[part], sems.at[pieces + at]))
    copies.append(pltpu.make_async_copy(wd.at[0], wd_in, sems.at[2 * pieces]))
    for copy in copies:
        copy.start()
    for copy in copies[:count]:
        copy.wait()
    for at in range(pieces):
        part = slice(at * piece, (at + 1) * piece)
        copies[count + 2 * at].wait()
        copies[count + 2 * at + 1].wait()
        rows = jnp.concatenate([x[n, :, part] for n in range(count)], axis=0)
        g = jnp.dot(rows, wg_in[part], preferred_element_type=F32)
        u = jnp.dot(rows, wu_in[part], preferred_element_type=F32)
        gate[...] = g if at == 0 else gate[...] + g
        up[...] = u if at == 0 else up[...] + u
    g = gate[...]
    hidden = (g / (1.0 + jnp.exp(-g)) * up[...]).astype(BF16)
    copies[-1].wait()
    out_piece = min(width, 1024)
    for at in range(0, width, out_piece):
        y = jnp.dot(hidden, wd_in[:, at : at + out_piece], preferred_element_type=F32)
        for n, r in enumerate(outs):
            r[:, at : at + out_piece] = y[n * height : (n + 1) * height].astype(BF16)


def expert(blocks, w_gate, w_up, w_down, events=()):
    count = len(blocks)
    height, width = blocks[0].shape
    depth = w_gate.shape[2]
    pieces = 8 if width % 2048 == 0 else 1
    anywhere = pl.BlockSpec(memory_space=pl.ANY)
    return pl.pallas_call(
        functools.partial(expert_kernel, count, pieces),
        in_specs=[anywhere] * (count + 3 + len(events)),
        out_specs=[pl.BlockSpec(memory_space=pltpu.VMEM)] * count,
        out_shape=[jax.ShapeDtypeStruct((height, width), BF16)] * count,
        scratch_shapes=[
            pltpu.VMEM((count, height, width), BF16),
            pltpu.VMEM((width, depth), BF16),
            pltpu.VMEM((width, depth), BF16),
            pltpu.VMEM((depth, width), BF16),
            pltpu.VMEM((count * height, depth), F32),
            pltpu.VMEM((count * height, depth), F32),
            pltpu.SemaphoreType.DMA((2 * pieces + 1,)),
            pltpu.SemaphoreType.DMA((count,)),
        ],
        compiler_params=pltpu.CompilerParams(vmem_limit_bytes=VMEM_LIMIT),
        cost_estimate=LONG,
        name="expert",
    )(*blocks, w_gate, w_up, w_down, *events)


def local(grid, tokens, routes, gates, w_gate, w_up, w_down):
    tok_rows, width = tokens.shape
    fanout = routes.shape[1]
    cap = tok_rows * fanout * 5 // (4 * grid.count)
    a, c = grid.side, grid.cores
    relays, returns = grid.relays(), grid.returns()

    table = np.zeros((grid.count, a * c), np.int32)
    for z in range(grid.seq):
        for p in range(grid.plane):
            table[z * grid.plane + p] = [z * grid.plane + grid.second(p, b, kc) for b in range(a) for kc in range(c)]
    ids = lax.dynamic_index_in_dim(jnp.asarray(table), lax.axis_index(AXES), 0, keepdims=False)

    hop1 = [None] + [grid.in_plane(lambda p, b=b: grid.first(p, b)) for b in range(1, a)]
    hop2 = [grid.in_plane(lambda p, b=b, kc=kc: grid.second(p, b, kc)) for b in range(a) for kc in range(c)]

    lines = 2 * fanout
    meta = jnp.concatenate([routes.astype(BF16), gates], axis=1).T
    meta = jnp.pad(meta, ((0, tok_rows - lines), (0, 0)))
    tokens = jnp.concatenate([tokens, meta], axis=1)

    seq_index = lax.axis_index("seq")
    last = grid.seq - 1
    held, known, rows, outs, returned = {0: tokens}, {}, {}, {}, {}
    steps, inbox, sums, parts = {}, [], {}, {}

    def land(values, event, us=0):
        if any(v is event for v in values):
            return values, event
        values = pin(values, event, us)
        return values, values[0]

    def send_near(s):
        known[s] = [held[s]] + [move(held[s], hop1[b]) for b in range(1, a)]

    def land_near(s, event):
        known[s][1:], event = land(known[s][1:], event)
        return event

    def begin(origin):
        for s in range(1, grid.seq):
            if relays[s][0][0] == origin:
                steps[s] = move(held[origin], grid.along_seq(relays[s][0][1]))

    def forward(s, event):
        if s > last or len(relays[s]) == 1:
            return event
        (first,), event = land([steps[s]], event)
        steps[s] = (first, move(first, grid.along_seq(relays[s][1][1])))
        return event

    def hold(s, event):
        if isinstance(steps[s], tuple):
            (second,), event = land([steps[s][1]], event)
            reached = functools.reduce(jnp.logical_or, [seq_index == d for _, d in relays[s][1][1]])
            held[s] = jnp.where(reached, second, steps[s][0])
        else:
            (held[s],), event = land([steps[s]], event)
        send_near(s)
        begin(s)
        return event

    def choose(s, event):
        chosen = select(grid, cap, ids, lines, width, known[s], [event])
        rows[s] = [chosen[0]] + [move(chosen[n], hop2[n]) for n in range(1, a * c)]
        return chosen[0]

    def land_inside(s, event):
        if c > 1:
            rows[s][1:c], event = land(rows[s][1:c], event)
        return event

    def land_rows(s, event):
        rows[s][c:], event = land(rows[s][c:], event, 8)
        return event

    def work(s, event):
        outs[s] = expert(rows[s], w_gate, w_up, w_down, [event])
        return outs[s][0]

    def give(s, event):
        values, event = land(outs[s], event)
        returned[s] = [values[0]] + [move(values[n], back(hop2[n])) for n in range(1, a * c)]
        return event

    def land_returned(s, event):
        returned[s][1:], event = land(returned[s][1:], event)
        return event

    def gather(s, event):
        values = mix(grid, cap, ids, lines, known[s], returned[s], list(range(1, a)), (), [event])
        sums[s] = [move(x, hop1[b + 1]) for b, x in enumerate(values)]
        return values[0]

    def finish(s, event):
        extras, event = land(sums[s] + (inbox if s == 0 else []), event)
        (parts[s],) = mix(grid, cap, ids, lines, known[s], returned[s], [0], extras, [event])
        return parts[s]

    def climb(s, event):
        (parts[s],), event = land([parts[s]], event)
        arrived = move(parts[s], grid.along_seq(returns[s][0]))
        if len(returns[s]) == 1:
            inbox.append(arrived)
        else:
            sums[s] = arrived
        return event

    def climb_on(s, event):
        if len(returns[s]) > 1:
            (arrived,), event = land([sums[s]], event)
            part = (parts[s].astype(F32) + arrived.astype(F32)).astype(BF16)
            inbox.append(move(part, grid.along_seq(returns[s][1])))
        return event

    send_near(0)
    begin(0)
    event = land_near(0, ids)
    event = choose(0, event)
    event = land_inside(0, event)
    for s in range(1, grid.seq):
        event = hold(s, event)
        event = forward(s + 1, event)
        if s > 1:
            event = land_inside(s - 1, event)
        if s > 1:
            event = work(s - 2, event)
        event = land_rows(s - 1, event)
        event = land_near(s, event)
        event = choose(s, event)
    event = work(last - 1, event)
    event = give(last - 1, event)
    event = land_inside(last, event)
    event = land_rows(last, event)
    event = work(last, event)
    event = give(last, event)
    event = land_returned(last - 1, event)
    event = gather(last - 1, event)
    event = land_returned(last, event)
    event = gather(last, event)
    event = finish(last - 1, event)
    event = climb(last - 1, event)
    event = give(last - 2, event)
    event = finish(last, event)
    event = climb(last, event)
    for s in range(last - 2, -1, -1):
        event = land_returned(s, event)
        event = gather(s, event)
        if s > 0:
            if s == last - 2:
                event = climb_on(last - 1, event)
            event = finish(s, event)
            event = climb(s, event)
            if s == last - 2:
                event = climb_on(last, event)
            event = give(s - 1, event)
    if grid.seq == 4:
        inbox[0:1], event = land(inbox[0:1], event)
    finish(0, event)
    return parts[0]


def solution(mesh):
    grid = Grid(mesh.shape["seq"], mesh.shape["expert"])
    two, three = P(AXES, None), P(AXES, None, None)
    return jax.shard_map(
        functools.partial(local, grid),
        mesh=mesh,
        in_specs=(two, two, two, three, three, three),
        out_specs=two,
        check_vma=False,
    )
```

```python
import functools
import math

import jax
import jax.numpy as jnp
import numpy as np
from jax import lax
from jax.experimental import pallas as pl
from jax.experimental.pallas import tpu as pltpu
from jax.sharding import PartitionSpec as P

AXES = ("seq", "expert")
F32 = jnp.float32
BF16 = jnp.bfloat16
VMEM_LIMIT = 56 * 1024 * 1024
TILE = 2048
SHORT = pl.CostEstimate(flops=2_000_000_000, bytes_accessed=6_000_000, transcendentals=0)
LONG = pl.CostEstimate(flops=6_000_000_000, bytes_accessed=24_000_000, transcendentals=0)


class Grid:
    def __init__(self, seq, plane):
        side = math.isqrt(plane)
        if side * side == plane:
            self.cores = 1
        else:
            self.cores = 2
            side = math.isqrt(plane // 2)
        self.seq, self.plane, self.side = seq, plane, side
        self.count = seq * plane

    def split(self, p):
        k = p % self.cores
        return p // self.cores // self.side, p // self.cores % self.side, k

    def join(self, i, j, k):
        return (i * self.side + j) * self.cores + k

    def first(self, p, b):
        i, j, k = self.split(p)
        return self.join(i, j ^ b, k) if k % 2 == 0 else self.join(i ^ b, j, k)

    def second(self, p, b, kc):
        i, j, k = self.split(p)
        return self.join(i ^ b, j, k ^ kc) if k % 2 == 0 else self.join(i, j ^ b, k ^ kc)

    def in_plane(self, move):
        return [(z * self.plane + p, z * self.plane + move(p)) for z in range(self.seq) for p in range(self.plane)]

    def along_seq(self, pairs):
        return [(s * self.plane + p, d * self.plane + p) for s, d in pairs for p in range(self.plane)]

    def relays(self):
        if self.seq == 4:
            near, middle, ends = [(0, 1), (1, 0), (2, 3), (3, 2)], [(1, 2), (2, 1)], [(1, 0), (2, 3)]
            return [[], [(0, near)], [(0, middle), (2, ends)], [(1, middle), (3, ends)]]
        return [[]] + [[(0, [(z, z ^ s) for z in range(self.seq)])] for s in range(1, self.seq)]


    def returns(self):
        if self.seq == 4:
            near, middle, ends = [(0, 1), (1, 0), (2, 3), (3, 2)], [(1, 2), (2, 1)], [(0, 1), (3, 2)]
            return [[], [near], [ends, middle], [ends, [(1, 3), (2, 0)]]]
        return [[]] + [[[(z, z ^ s) for z in range(self.seq)]] for s in range(1, self.seq)]


def back(pairs):
    return [(d, s) for s, d in pairs]


def move(x, pairs):
    return lax.ppermute(x, AXES, pairs)


def pin_kernel(*refs):
    pass


def pin(values, event, us=0):
    count = len(values)
    anywhere = pl.BlockSpec(memory_space=pl.ANY)
    return pl.pallas_call(
        pin_kernel,
        in_specs=[anywhere] * (count + 1),
        out_specs=[anywhere] * count,
        out_shape=[jax.ShapeDtypeStruct(v.shape, v.dtype) for v in values],
        input_output_aliases={n: n for n in range(count)},
        cost_estimate=pl.CostEstimate(flops=int(us * 1e9), bytes_accessed=int(us * 3e6), transcendentals=0),
        name="pin",
    )(*values, event)


def codes(meta, experts, base, want_gates):
    meta = meta.astype(F32)
    fanout = meta.shape[0] // 2
    tokens = meta.shape[1]
    routes, gates = meta[:fanout], meta[fanout:]
    height = -(-len(experts) // 8) * 8
    line = lax.broadcasted_iota(jnp.int32, (height, tokens), 0)
    named = jnp.zeros((height, tokens), F32)
    weights = jnp.zeros((height, tokens), F32)
    for n, e in enumerate(experts):
        hit = routes == e.astype(F32)
        named = jnp.where(line == n, jnp.max(jnp.where(hit, 1.0, 0.0), axis=0, keepdims=True), named)
        if want_gates:
            weights = jnp.where(line == n, jnp.sum(jnp.where(hit, gates, 0.0), axis=0, keepdims=True), weights)
    before = lax.broadcasted_iota(jnp.int32, (tokens, tokens), 0) < lax.broadcasted_iota(jnp.int32, (tokens, tokens), 1)
    rank = jnp.dot(named.astype(BF16), jnp.where(before, 1.0, 0.0).astype(BF16), preferred_element_type=F32)
    return jnp.where(named > 0, rank + base, -1.0), weights


def select_kernel(grid, cap, ids, *refs):
    a, outs = grid.side, grid.side * grid.cores
    metas, toks, results, table = refs[:a], refs[a : 2 * a], refs[-outs - 1 : -1], refs[-1]

    @pl.when(pl.program_id(0) == 0)
    def _():
        experts = [ids[n] for n in range(outs)]
        for src in range(a):
            rows, _ = codes(metas[src][...], experts, src * cap, False)
            line = lax.broadcasted_iota(jnp.int32, (a * cap, rows.shape[1]), 0).astype(F32)
            for n in range(outs):
                table[src, n] = jnp.where(line == rows[n : n + 1], 1.0, 0.0).astype(BF16)

    for n in range(outs):
        total = jnp.dot(table[0, n], toks[0][...], preferred_element_type=F32)
        for src in range(1, a):
            total = total + jnp.dot(table[src, n], toks[src][...], preferred_element_type=F32)
        results[n][...] = total.astype(BF16)


def meta_spec(tok, width, lines):
    rows = tok.shape[0]
    return pl.BlockSpec((lines, rows), lambda d, ids: (0, width // rows))


def select(grid, cap, ids, lines, width, toks, events=()):
    a, outs = grid.side, grid.side * grid.cores
    rows = toks[0].shape[0]
    tile = min(width, TILE)
    return pl.pallas_call(
        functools.partial(select_kernel, grid, cap),
        grid_spec=pltpu.PrefetchScalarGridSpec(
            num_scalar_prefetch=1,
            grid=(width // tile,),
            in_specs=[meta_spec(tok, width, lines) for tok in toks]
            + [pl.BlockSpec((rows, tile), lambda d, ids: (0, d)) for _ in range(a)]
            + [pl.BlockSpec(memory_space=pl.ANY) for _ in events],
            out_specs=[pl.BlockSpec((a * cap, tile), lambda d, ids: (0, d)) for _ in range(outs)],
            scratch_shapes=[pltpu.VMEM((a, outs, a * cap, rows), BF16)],
        ),
        out_shape=[jax.ShapeDtypeStruct((a * cap, width), BF16) for _ in range(outs)],
        compiler_params=pltpu.CompilerParams(vmem_limit_bytes=VMEM_LIMIT),
        cost_estimate=SHORT,
        name="select",
    )(ids, *toks, *toks, *events)


def mix_kernel(grid, cap, sources, extras, ids, *refs):
    a, ins = grid.side, grid.side * grid.cores
    metas, refs = refs[: len(sources)], refs[len(sources) :]
    blocks, refs = refs[:ins], refs[ins:]
    added, results, table = refs[:extras], refs[-len(sources) - 1 : -1], refs[-1]

    @pl.when(pl.program_id(0) == 0)
    def _():
        experts = [ids[n] for n in range(ins)]
        for at, src in enumerate(sources):
            rows, weights = codes(metas[at][...], experts, src * cap, True)
            rows, weights = rows.T, weights.T
            line = lax.broadcasted_iota(jnp.int32, (rows.shape[0], a * cap), 1).astype(F32)
            for n in range(ins):
                spread = jnp.where(line == rows[:, n : n + 1], weights[:, n : n + 1], 0.0)
                table[at, n] = spread.astype(BF16)

    for at in range(len(sources)):
        total = jnp.dot(table[at, 0], blocks[0][...], preferred_element_type=F32)
        for n in range(1, ins):
            total = total + jnp.dot(table[at, n], blocks[n][...], preferred_element_type=F32)
        for ref in added:
            total = total + ref[...].astype(F32)
        results[at][...] = total.astype(BF16)


def mix(grid, cap, ids, lines, toks, blocks, sources, extras=(), events=()):
    a, ins = grid.side, grid.side * grid.cores
    rows, width = toks[0].shape[0], blocks[0].shape[1]
    tile = min(width, TILE)
    wide = pl.BlockSpec((rows, tile), lambda d, ids: (0, d))
    return pl.pallas_call(
        functools.partial(mix_kernel, grid, cap, sources, len(extras)),
        grid_spec=pltpu.PrefetchScalarGridSpec(
            num_scalar_prefetch=1,
            grid=(width // tile,),
            in_specs=[meta_spec(toks[src], width, lines) for src in sources]
            + [pl.BlockSpec((a * cap, tile), lambda d, ids: (0, d)) for _ in blocks]
            + [wide for _ in extras]
            + [pl.BlockSpec(memory_space=pl.ANY) for _ in events],
            out_specs=[wide for _ in sources],
            scratch_shapes=[pltpu.VMEM((len(sources), ins, rows, a * cap), BF16)],
        ),
        out_shape=[jax.ShapeDtypeStruct((rows, width), BF16) for _ in sources],
        compiler_params=pltpu.CompilerParams(vmem_limit_bytes=VMEM_LIMIT),
        cost_estimate=SHORT,
        name="mix",
    )(ids, *[toks[src] for src in sources], *blocks, *extras, *events)


def expert_kernel(count, pieces, *refs):
    ins, (wg, wu, wd), outs = refs[:count], refs[count : count + 3], refs[-count - 8 : -8]
    x, wg_in, wu_in, wd_in, gate, up, sems, x_sems = refs[-8:]
    height = ins[0].shape[0]
    width, depth = wg.shape[1:]
    piece = width // pieces
    copies = []
    for n, r in enumerate(ins):
        copies.append(pltpu.make_async_copy(r, x.at[n], x_sems.at[n]))
    for at in range(pieces):
        part = pl.ds(at * piece, piece)
        copies.append(pltpu.make_async_copy(wg.at[0, part], wg_in.at[part], sems.at[at]))
        copies.append(pltpu.make_async_copy(wu.at[0, part], wu_in.at[part], sems.at[pieces + at]))
    copies.append(pltpu.make_async_copy(wd.at[0], wd_in, sems.at[2 * pieces]))
    for copy in copies:
        copy.start()
    for copy in copies[:count]:
        copy.wait()
    for at in range(pieces):
        part = slice(at * piece, (at + 1) * piece)
        copies[count + 2 * at].wait()
        copies[count + 2 * at + 1].wait()
        rows = jnp.concatenate([x[n, :, part] for n in range(count)], axis=0)
        g = jnp.dot(rows, wg_in[part], preferred_element_type=F32)
        u = jnp.dot(rows, wu_in[part], preferred_element_type=F32)
        gate[...] = g if at == 0 else gate[...] + g
        up[...] = u if at == 0 else up[...] + u
    g = gate[...]
    hidden = (g / (1.0 + jnp.exp(-g)) * up[...]).astype(BF16)
    copies[-1].wait()
    out_piece = min(width, 1024)
    for at in range(0, width, out_piece):
        y = jnp.dot(hidden, wd_in[:, at : at + out_piece], preferred_element_type=F32)
        for n, r in enumerate(outs):
            r[:, at : at + out_piece] = y[n * height : (n + 1) * height].astype(BF16)


def expert(blocks, w_gate, w_up, w_down, events=()):
    count = len(blocks)
    height, width = blocks[0].shape
    depth = w_gate.shape[2]
    pieces = 8 if width % 2048 == 0 else 1
    anywhere = pl.BlockSpec(memory_space=pl.ANY)
    return pl.pallas_call(
        functools.partial(expert_kernel, count, pieces),
        in_specs=[anywhere] * (count + 3 + len(events)),
        out_specs=[pl.BlockSpec(memory_space=pltpu.VMEM)] * count,
        out_shape=[jax.ShapeDtypeStruct((height, width), BF16)] * count,
        scratch_shapes=[
            pltpu.VMEM((count, height, width), BF16),
            pltpu.VMEM((width, depth), BF16),
            pltpu.VMEM((width, depth), BF16),
            pltpu.VMEM((depth, width), BF16),
            pltpu.VMEM((count * height, depth), F32),
            pltpu.VMEM((count * height, depth), F32),
            pltpu.SemaphoreType.DMA((2 * pieces + 1,)),
            pltpu.SemaphoreType.DMA((count,)),
        ],
        compiler_params=pltpu.CompilerParams(vmem_limit_bytes=VMEM_LIMIT),
        cost_estimate=LONG,
        name="expert",
    )(*blocks, w_gate, w_up, w_down, *events)


def local(grid, tokens, routes, gates, w_gate, w_up, w_down):
    tok_rows, width = tokens.shape
    fanout = routes.shape[1]
    cap = tok_rows * fanout * 5 // (4 * grid.count)
    a, c = grid.side, grid.cores
    relays, returns = grid.relays(), grid.returns()

    table = np.zeros((grid.count, a * c), np.int32)
    for z in range(grid.seq):
        for p in range(grid.plane):
            table[z * grid.plane + p] = [z * grid.plane + grid.second(p, b, kc) for b in range(a) for kc in range(c)]
    ids = lax.dynamic_index_in_dim(jnp.asarray(table), lax.axis_index(AXES), 0, keepdims=False)

    hop1 = [None] + [grid.in_plane(lambda p, b=b: grid.first(p, b)) for b in range(1, a)]
    hop2 = [grid.in_plane(lambda p, b=b, kc=kc: grid.second(p, b, kc)) for b in range(a) for kc in range(c)]

    lines = 2 * fanout
    meta = jnp.concatenate([routes.astype(BF16), gates], axis=1).T
    meta = jnp.pad(meta, ((0, tok_rows - lines), (0, 0)))
    tokens = jnp.concatenate([tokens, meta], axis=1)

    seq_index = lax.axis_index("seq")
    last = grid.seq - 1
    held, known, rows, outs, returned = {0: tokens}, {}, {}, {}, {}
    steps, inbox, sums, parts = {}, [], {}, {}

    def land(values, event, us=0):
        if any(v is event for v in values):
            return values, event
        values = pin(values, event, us)
        return values, values[0]

    def send_near(s):
        known[s] = [held[s]] + [move(held[s], hop1[b]) for b in range(1, a)]

    def land_near(s, event):
        known[s][1:], event = land(known[s][1:], event)
        return event

    def begin(origin):
        for s in range(1, grid.seq):
            if relays[s][0][0] == origin:
                steps[s] = move(held[origin], grid.along_seq(relays[s][0][1]))

    def forward(s, event):
        if s > last or len(relays[s]) == 1:
            return event
        (first,), event = land([steps[s]], event)
        steps[s] = (first, move(first, grid.along_seq(relays[s][1][1])))
        return event

    def hold(s, event):
        if isinstance(steps[s], tuple):
            (second,), event = land([steps[s][1]], event)
            reached = functools.reduce(jnp.logical_or, [seq_index == d for _, d in relays[s][1][1]])
            held[s] = jnp.where(reached, second, steps[s][0])
        else:
            (held[s],), event = land([steps[s]], event)
        send_near(s)
        begin(s)
        return event

    def choose(s, event):
        chosen = select(grid, cap, ids, lines, width, known[s], [event])
        rows[s] = [chosen[0]] + [move(chosen[n], hop2[n]) for n in range(1, a * c)]
        return chosen[0]

    def land_inside(s, event):
        if c > 1:
            rows[s][1:c], event = land(rows[s][1:c], event)
        return event

    def land_rows(s, event):
        rows[s][c:], event = land(rows[s][c:], event, 8)
        return event

    def work(s, event):
        outs[s] = expert(rows[s], w_gate, w_up, w_down, [event])
        return outs[s][0]

    def give(s, event):
        values, event = land(outs[s], event)
        returned[s] = [values[0]] + [move(values[n], back(hop2[n])) for n in range(1, a * c)]
        return event

    def land_returned(s, event):
        returned[s][1:], event = land(returned[s][1:], event)
        return event

    def gather(s, event):
        values = mix(grid, cap, ids, lines, known[s], returned[s], list(range(1, a)), (), [event])
        sums[s] = [move(x, hop1[b + 1]) for b, x in enumerate(values)]
        return values[0]

    def finish(s, event):
        extras, event = land(sums[s] + (inbox if s == 0 else []), event)
        (parts[s],) = mix(grid, cap, ids, lines, known[s], returned[s], [0], extras, [event])
        return parts[s]

    def climb(s, event):
        (parts[s],), event = land([parts[s]], event)
        arrived = move(parts[s], grid.along_seq(returns[s][0]))
        if len(returns[s]) == 1:
            inbox.append(arrived)
        else:
            sums[s] = arrived
        return event

    def climb_on(s, event):
        if len(returns[s]) > 1:
            (arrived,), event = land([sums[s]], event)
            part = (parts[s].astype(F32) + arrived.astype(F32)).astype(BF16)
            inbox.append(move(part, grid.along_seq(returns[s][1])))
        return event

    send_near(0)
    begin(0)
    event = land_near(0, ids)
    event = choose(0, event)
    event = land_inside(0, event)
    for s in range(1, grid.seq):
        event = hold(s, event)
        event = forward(s + 1, event)
        if s > 1:
            event = land_inside(s - 1, event)
        if s > 1:
            event = work(s - 2, event)
        event = land_rows(s - 1, event)
        event = land_near(s, event)
        event = choose(s, event)
    event = work(last - 1, event)
    event = give(last - 1, event)
    event = land_inside(last, event)
    event = land_rows(last, event)
    event = work(last, event)
    event = give(last, event)
    event = land_returned(last - 1, event)
    event = gather(last - 1, event)
    event = land_returned(last, event)
    event = gather(last, event)
    event = finish(last - 1, event)
    event = climb(last - 1, event)
    event = give(last - 2, event)
    event = finish(last, event)
    event = climb(last, event)
    for s in range(last - 2, -1, -1):
        event = land_returned(s, event)
        event = gather(s, event)
        if s > 0:
            if s == last - 2:
                event = climb_on(last - 1, event)
            event = finish(s, event)
            event = climb(s, event)
            event = give(s - 1, event)
            if s == last - 2:
                event = climb_on(last, event)
    if grid.seq == 4:
        inbox[0:1], event = land(inbox[0:1], event)
    finish(0, event)
    return parts[0]


def solution(mesh):
    grid = Grid(mesh.shape["seq"], mesh.shape["expert"])
    two, three = P(AXES, None), P(AXES, None, None)
    return jax.shard_map(
        functools.partial(local, grid),
        mesh=mesh,
        in_specs=(two, two, two, three, three, three),
        out_specs=two,
        check_vma=False,
    )
```
